128 devices in a mesh: wide: 16 (over z, x), narrow: 8 (over y, core).
Axes of the slice: x: 4, y: 4, z: 4, core: 2. Of those that a mesh axis runs over, the one named last changes fastest.
Arguments:
- cotangent: float32 [1536, 256, 256], P(('wide', 'narrow')), may hold values from -6 to 6
- row_basis: float32 [1536, 256, 128], P(('wide', 'narrow')), may hold values from -0.375 to 0.375
- col_basis: float32 [1536, 256, 128], P(('wide', 'narrow')), may hold values from -0.5 to 0.5
- leaf_up: float32 [1536, 128, 128], P(('wide', 'narrow')), may hold values from -0.15625 to 0.15625
- node_up: float32 [128, 128, 128], P(('wide', 'narrow')), may hold values from -0.1875 to 0.1875
- node_couple: float32 [128, 2, 128, 128], P(('wide', 'narrow')), may hold values from -0.375 to 0.375
- group_couple: float32 [16, 8, 128, 128], P('wide', 'narrow'), may hold values from -0.1875 to 0.1875
- node_down: float32 [128, 128, 128], P(('wide', 'narrow')), may hold values from -0.5 to 0.5
- leaf_down: float32 [1536, 128, 128], P(('wide', 'narrow')), may hold values from -0.5 to 0.5
- near_blocks: float32 [1536, 4, 256, 256], P(('wide', 'narrow')), may hold values from -0.1875 to 0.1875
- near_index: int32 [1536, 4], P(('wide', 'narrow')), may hold values from 0 to 1535, as said below
- far_nodes: int32 [128, 2], P(('wide', 'narrow')), may hold values from 0 to 7, as said below
- far_groups: int32 [16, 8], P('wide', 'narrow'), may hold values from 0 to 15, as said below
Outputs:
- product: float32 [1536, 256, 256], P(('wide', 'narrow'))
The draws below stay inside these ranges and needn't reach their ends.
Inputs may be any that keep to these rules, and one draw needn't show every extreme that they name: near_index[l, 0] is l; every other entry differs from l by 1 to 2. far_nodes[d, j] never equals d % 8; the entries of a row differ. far_groups[g, j] never equals g; the entries of a row differ.
All inputs are finite; a program needn't handle non-finite values.
Results may differ from the reference program's by a relative error of at most 0.000062.
Values sent between devices are 32-bit elements; how exact they have to be, the bound alone decides.
A program may use at most 128 MiB of HBM per device.

```python
import jax
import jax.numpy as jnp
from jax import lax

PTS = 256
RANK = 128
NVEC = 256
LEAF_DEV = 12
NNEAR = 4
NEAR_REACH = 2
NFAR1 = 2
GROUPS = 16
SIBLINGS = 8
NODES = 128
NLEAF = 1536
NFAR2 = 8
N_NARROW = 8


def draw_near_index(key, part):
    leaves = jnp.arange(NLEAF, dtype=jnp.int32)
    keys = jax.random.split(key, NLEAF)
    orders = jax.vmap(lambda k: jax.random.permutation(k, 2 * NEAR_REACH))(keys)[:, :NNEAR - 1].astype(jnp.int32)
    offsets = jnp.where(orders < NEAR_REACH, orders - NEAR_REACH, orders - NEAR_REACH + 1)
    target = leaves[:, None] + offsets
    target = jnp.where((target < 0) | (target >= NLEAF), leaves[:, None] - offsets, target)
    return jnp.concatenate([leaves[:, None], target], axis=1).astype(jnp.int32)


def draw_far_nodes(key, part):
    position = jnp.arange(NODES, dtype=jnp.int32) % SIBLINGS
    keys = jax.random.split(key, NODES)
    orders = jax.vmap(lambda k: jax.random.permutation(k, SIBLINGS - 1))(keys)[:, :NFAR1].astype(jnp.int32)
    return ((position[:, None] + orders + 1) % SIBLINGS).astype(jnp.int32)


def draw_far_groups(key, part):
    groups = jnp.arange(GROUPS, dtype=jnp.int32)
    keys = jax.random.split(key, GROUPS)
    orders = jax.vmap(lambda k: jax.random.permutation(k, GROUPS - 1))(keys)[:, :NFAR2].astype(jnp.int32)
    return ((groups[:, None] + orders + 1) % GROUPS).astype(jnp.int32)


def level_of(own_key, dims, pieces, low, largest):
    level, own = 1.0, jax.random.fold_in(own_key, 6)
    for dim, parts in pieces:
        draws = jnp.exp(jax.random.uniform(jax.random.fold_in(own, dim), (parts,), jnp.float32, low / len(pieces), largest / len(pieces)))
        level = level * jnp.repeat(draws, dims[dim] // parts).reshape([-1 if axis == dim else 1 for axis in range(len(dims))])
    return level


def scatter_about(stream_key, dims, width, limit, cuts=(), kind=jnp.bfloat16):
    drawn = jax.random.normal(stream_key, dims, jnp.float32) * width
    if len(cuts) > 0:
        drawn = level_of(stream_key, dims, cuts, -0.22, 0.18) * drawn
    return jnp.clip(drawn, min=-limit, max=limit).astype(kind)


def setup_inputs(seed: int = 0) -> dict:
    streams_of = jax.random.split(jax.random.key(seed), 14)
    return {
        "cotangent": scatter_about(streams_of[0], (NLEAF, PTS, NVEC), 1.0, 6.0, ((0, 128),), jnp.float32),
        "row_basis": scatter_about(streams_of[1], (NLEAF, PTS, RANK), PTS ** -0.5, 0.375, ((0, 128),), jnp.float32),
        "col_basis": scatter_about(streams_of[2], (NLEAF, PTS, RANK), RANK ** -0.5, 0.5, ((0, 128),), jnp.float32),
        "leaf_up": scatter_about(streams_of[3], (NLEAF, RANK, RANK), (RANK * LEAF_DEV) ** -0.5, 0.15625, ((0, 128),), jnp.float32),
        "node_up": scatter_about(streams_of[4], (NODES, RANK, RANK), (RANK * N_NARROW) ** -0.5, 0.1875, ((0, 128),), jnp.float32),
        "node_couple": scatter_about(streams_of[5], (NODES, NFAR1, RANK, RANK), (RANK * NFAR1) ** -0.5, 0.375, ((0, 128),), jnp.float32),
        "group_couple": scatter_about(streams_of[6], (GROUPS, NFAR2, RANK, RANK), (RANK * NFAR2) ** -0.5, 0.1875, ((0, 16), (1, 8)), jnp.float32),
        "node_down": scatter_about(streams_of[7], (NODES, RANK, RANK), RANK ** -0.5, 0.5, ((0, 128),), jnp.float32),
        "leaf_down": scatter_about(streams_of[8], (NLEAF, RANK, RANK), RANK ** -0.5, 0.5, ((0, 128),), jnp.float32),
        "near_blocks": scatter_about(streams_of[9], (NLEAF, NNEAR, PTS, PTS), (PTS * NNEAR) ** -0.5, 0.1875, ((0, 128),), jnp.float32),
        "near_index": draw_near_index(jax.random.fold_in(streams_of[13], 71), 0),
        "far_nodes": draw_far_nodes(jax.random.fold_in(streams_of[13], 71), 0),
        "far_groups": draw_far_groups(jax.random.fold_in(streams_of[13], 71), 0),
    }


HIGH = lax.Precision.HIGHEST


def reference(cotangent, row_basis, col_basis, leaf_up, node_up, node_couple, group_couple, node_down, leaf_down, near_blocks, near_index, far_nodes, far_groups):
    leaf_coeffs = jnp.einsum('lpk,lpv->lkv', row_basis, cotangent, precision=HIGH)
    up_terms = jnp.einsum('lkm,lkv->lmv', leaf_up, leaf_coeffs, precision=HIGH)
    node_coeffs = jnp.sum(up_terms.reshape(NODES, LEAF_DEV, RANK, NVEC), axis=1)
    group_terms = jnp.einsum('dkm,dkv->dmv', node_up, node_coeffs, precision=HIGH)
    group_coeffs = jnp.sum(group_terms.reshape(GROUPS, SIBLINGS, RANK, NVEC), axis=1)
    base = (jnp.arange(NODES, dtype=jnp.int32) // SIBLINGS) * SIBLINGS
    picked = node_coeffs[(base[:, None] + far_nodes).astype(jnp.int32)]
    node_out = jnp.einsum('djkm,djkv->dmv', node_couple, picked, precision=HIGH)
    picked_groups = group_coeffs[far_groups]
    group_out = jnp.einsum('gjkm,gjkv->gmv', group_couple, picked_groups, precision=HIGH)
    group_of = jnp.repeat(group_out, SIBLINGS, axis=0)
    node_total = node_out + jnp.einsum('dmk,dkv->dmv', node_down, group_of, precision=HIGH)
    node_of = jnp.repeat(node_total, LEAF_DEV, axis=0)
    leaf_total = jnp.einsum('lmk,lkv->lmv', leaf_down, node_of, precision=HIGH)
    far_part = jnp.einsum('lpk,lkv->lpv', col_basis, leaf_total, precision=HIGH)

    def near_node(args):
        blocks, index = args
        sources = cotangent[index]
        return jnp.einsum('ljpq,ljpv->lqv', blocks, sources, precision=HIGH)

    near_part = lax.map(near_node, (near_blocks.reshape(NODES, LEAF_DEV, NNEAR, PTS, PTS), near_index.reshape(NODES, LEAF_DEV, NNEAR)))
    return far_part + near_part.reshape(NLEAF, PTS, NVEC)
```

```python
import functools

import jax
import jax.numpy as jnp
from jax import lax
from jax.experimental import pallas as pl
from jax.experimental.pallas import tpu as pltpu
from jax.sharding import PartitionSpec as P

MESH = pl.DeviceIdType.MESH
F32, BF16 = jnp.float32, jnp.bfloat16
LEAVES, PTS, RANK, NVEC = 12, 256, 128, 256
REACH, NNEAR = 2, 4
WIDE, NARROW, SIDE = 16, 8, 4
SLICE = NVEC // NARROW
OFFSETS = [(dz, dx) for dz in (2, 1, 3, 0) for dx in (2, 1, 3, 0) if dz or dx]


def split(value):
    high = value.astype(BF16)
    return high, (value - high.astype(F32)).astype(BF16)


def dot(a, b, dims=((1,), (0,))):
    return lax.dot_general(a, b, (dims, ((), ())), preferred_element_type=F32)


def dot3(a, b, dims=((1,), (0,))):
    (ah, al), (bh, bl) = a, b
    return dot(ah, bh, dims) + (dot(al, bh, dims) + dot(ah, bl, dims))


def exchange(
    cot, rb, cb, lu, nu, nc, gc, nd, ld, nb, ni_hbm, fn_hbm, fg,
    near_out, mh_out, ml_out, nth_out, ntl_out,
    cotv, rbv, cbv, luv, nuv, ncv, gcv, ndv, ldv, nbv,
    cth, ctl, upv, sib, abuf, bbuf, cbuf, outv, ni, fn,
    leaf_sem, small_sem, cb_sem, nb_sem,
    sa, ra, sb, rb_, sc, rc, ss, rs, sg, rg, sh, rh, go, int_sem,
):
    w, n = lax.axis_index("wide"), lax.axis_index("narrow")
    core = lax.rem(n, 2)

    def mate(d):
        return w, lax.rem(n + d, NARROW)

    def far(dz, dx, sign):
        z = lax.rem(w // SIDE + SIDE + sign * dz, SIDE)
        x = lax.rem(lax.rem(w, SIDE) + SIDE + sign * dx, SIDE)
        return z * SIDE + x, n

    rank = w * NARROW + n
    after, before = lax.rem(rank + 1, WIDE * NARROW), lax.rem(rank + WIDE * NARROW - 1, WIDE * NARROW)
    after, before = (after // NARROW, lax.rem(after, NARROW)), (before // NARROW, lax.rem(before, NARROW))

    barrier = pltpu.get_barrier_semaphore()
    for dz, dx in OFFSETS:
        pl.semaphore_signal(barrier, inc=1, device_id=far(dz, dx, 1), device_id_type=MESH)
    for d in range(1, NARROW):
        pl.semaphore_signal(barrier, inc=1, device_id=mate(d), device_id_type=MESH)

    def leaf_copies(leaf):
        return [
            pltpu.make_async_copy(rb.at[leaf], rbv.at[leaf], leaf_sem.at[0, leaf]),
            pltpu.make_async_copy(lu.at[leaf], luv.at[leaf], leaf_sem.at[1, leaf]),
            pltpu.make_async_copy(cot.at[leaf], cotv.at[REACH + leaf], leaf_sem.at[2, leaf]),
        ]

    @pl.loop(0, LEAVES)
    def _(leaf):
        for c in leaf_copies(leaf):
            c.start()

    smalls = [
        pltpu.make_async_copy(nu.at[0], nuv, small_sem.at[0]),
        pltpu.make_async_copy(gc.at[0, 0], gcv.at[n, pl.ds(0, RANK)], small_sem.at[1]),
        pltpu.make_async_copy(nc.at[0], ncv, small_sem.at[2]),
        pltpu.make_async_copy(nd.at[0], ndv, small_sem.at[3]),
    ]
    ints = [
        pltpu.make_async_copy(a, b, int_sem.at[i])
        for i, (a, b) in enumerate(((ni_hbm, ni), (fn_hbm, fn)))
    ]
    for c in smalls + ints:
        c.start()
    for c in ints:
        c.wait()

    gcv[n, RANK:, :] = jnp.full((8, RANK), fg[0, 0].astype(F32), F32)
    upv[...] = jnp.zeros_like(upv)

    def prepare(slot):
        turned = cotv[slot].T
        high, low = split(turned)
        cth[slot], ctl[slot] = high, low
        return high, low

    @pl.loop(0, LEAVES)
    def _(leaf):
        for c in leaf_copies(leaf):
            c.wait()
        basis = dot3(split(rbv[leaf]), split(luv[leaf]))
        upv[...] += dot3(prepare(REACH + leaf), split(basis))

    near_copies = functools.partial(
        lambda leaf: pltpu.make_async_copy(nb.at[leaf], nbv.at[leaf], nb_sem.at[leaf])
    )
    late = [pltpu.make_async_copy(cb, cbv, cb_sem.at[0]), pltpu.make_async_copy(ld, ldv, cb_sem.at[1])]
    for c in late:
        c.start()

    @pl.loop(0, LEAVES)
    def _(leaf):
        near_copies(leaf).start()

    coeffs = upv[...]
    sib[n] = coeffs
    for c in smalls:
        c.wait()
    upv[...] = dot3(split(coeffs), split(nuv[...]))

    pl.semaphore_wait(barrier, len(OFFSETS) + NARROW - 1)

    first = []
    for d in range(1, NARROW):
        to = mate(d)
        first.append(
            pltpu.make_async_remote_copy(
                upv.at[pl.ds(pl.multiple_of(to[1] * SLICE, SLICE), SLICE)], abuf.at[d - 1],
                sa.at[d - 1], ra.at[d - 1], device_id=to, device_id_type=MESH,
            )
        )
        first[-1].start()

    @pl.when(n == NARROW - 1)
    def _():
        pl.semaphore_signal(go, inc=1, device_id=(lax.rem(w + WIDE - 1, WIDE), n), device_id_type=MESH)

    @pl.when(n == 0)
    def _():
        pl.semaphore_signal(go, inc=1, device_id=(lax.rem(w + 1, WIDE), n), device_id_type=MESH)

    twin = (w, n + 1 - 2 * core)

    def spread(buf, send, recv):
        out = []
        for step in range(SIDE):
            to = twin if step == 0 else mate(2 * step)
            out.append(
                pltpu.make_async_remote_copy(
                    buf.at[n], buf.at[n], send.at[step], recv.at[step], device_id=to, device_id_type=MESH
                )
            )
        return out

    def arrived(buf, send, recv, step):
        source = lax.rem(n + NARROW - 2 * step, NARROW)
        return pltpu.make_async_remote_copy(
            buf.at[source], buf.at[source], send.at[step], recv.at[step], device_id=twin, device_id_type=MESH
        )

    def relay(buf, send, recv, step):
        source = lax.rem(n + NARROW - 2 * step, NARROW)
        return pltpu.make_async_remote_copy(
            buf.at[source], buf.at[source], send.at[SIDE - 1 + step], recv.at[SIDE - 1 + step],
            device_id=twin, device_id_type=MESH,
        )

    groups = spread(gcv, sg, rg)
    for c in groups:
        c.start()
    siblings = spread(sib, ss, rs)
    for c in siblings:
        c.start()

    @pl.when((n == NARROW - 1) | (n == 0))
    def _():
        pl.semaphore_wait(go, 1)

    halo = [
        pltpu.make_async_remote_copy(
            cot.at[pl.ds(LEAVES - REACH, REACH)], cotv.at[pl.ds(0, REACH)],
            sh.at[0], rh.at[0], device_id=after, device_id_type=MESH,
        ),
        pltpu.make_async_remote_copy(
            cot.at[pl.ds(0, REACH)], cotv.at[pl.ds(REACH + LEAVES, REACH)],
            sh.at[1], rh.at[1], device_id=before, device_id_type=MESH,
        ),
    ]
    for c in halo:
        c.start()

    for c in late:
        c.wait()

    @pl.loop(0, LEAVES)
    def _(leaf):
        mh, ml = split(dot3(split(cbv[leaf]), split(ldv[leaf])))
        mh_out[leaf], ml_out[leaf] = mh, ml

    first_leaf = rank * LEAVES - REACH

    def near(leaf):
        near_copies(leaf).wait()
        total = None
        for j in range(NNEAR):
            source = jnp.clip(ni[j, leaf] - first_leaf, 0, LEAVES + 2 * REACH - 1)
            term = dot3((cth[source], ctl[source]), split(nbv[leaf, j]))
            total = term if total is None else total + term
        near_out[leaf] = total.T

    @pl.loop(2, 5)
    def _(leaf):
        near(leaf)

    own = upv[pl.ds(pl.multiple_of(n * SLICE, SLICE), SLICE), :]
    for d, c in enumerate(first):
        c.wait_recv()
        own += abuf[d]
    bbuf[w] = own
    second = []
    for i, (dz, dx) in enumerate(OFFSETS):
        second.append(
            pltpu.make_async_remote_copy(
                bbuf.at[w], bbuf.at[w], sb.at[i], rb_.at[i], device_id=far(dz, dx, 1), device_id_type=MESH
            )
        )
        second[-1].start()

    relays = []
    for step in range(1, SIDE):
        arrived(gcv, sg, rg, step).wait_recv()
        relays.append(relay(gcv, sg, rg, step))
        relays[-1].start()

    @pl.loop(5, 10)
    def _(leaf):
        near(leaf)

    for step in range(1, SIDE):
        arrived(sib, ss, rs, step).wait_recv()
        relays.append(relay(sib, ss, rs, step))
        relays[-1].start()

    def from_twin(buf, send, recv, step):
        at = 0 if step == 0 else SIDE - 1 + step
        source = lax.rem(twin[1] + NARROW - 2 * step, NARROW)
        return pltpu.make_async_remote_copy(
            buf.at[source], buf.at[source], send.at[at], recv.at[at], device_id=twin, device_id_type=MESH
        )

    for step in range(SIDE):
        from_twin(gcv, sg, rg, step).wait_recv()
    for i, (dz, dx) in enumerate(OFFSETS):
        source = far(dz, dx, -1)[0]
        pltpu.make_async_remote_copy(
            bbuf.at[source], bbuf.at[source], sb.at[i], rb_.at[i], device_id=far(dz, dx, 1), device_id_type=MESH
        ).wait_recv()

    part = jnp.zeros((SLICE, RANK), F32)
    for j in range(NARROW):
        tag = jnp.concatenate([gcv[j, RANK:, :]] * (SLICE // 8), axis=0)
        picked = bbuf[0]
        for g in range(1, WIDE):
            picked = jnp.where(tag == float(g), bbuf[g], picked)
        part += dot3(split(picked), split(gcv[j, :RANK, :]))
    mine = pl.ds(pl.multiple_of(n * SLICE, SLICE), SLICE)
    cbuf[mine, :] = part
    third = []
    for d in range(1, NARROW):
        third.append(
            pltpu.make_async_remote_copy(
                cbuf.at[mine], cbuf.at[mine], sc.at[d - 1], rc.at[d - 1], device_id=mate(d), device_id_type=MESH
            )
        )
        third[-1].start()

    for step in range(SIDE):
        from_twin(sib, ss, rs, step).wait_recv()
    node = jnp.zeros((NVEC, RANK), F32)
    for j in range(2):
        node += dot3(split(sib[jnp.clip(fn[0, j], 0, NARROW - 1)]), split(ncv[j]))
    outv[...] = node

    for c in halo:
        c.wait_recv()
    for slot in (0, 1, REACH + LEAVES, REACH + LEAVES + 1):
        prepare(slot)

    @pl.loop(0, 4)
    def _(i):
        near(i + jnp.where(i < 2, 0, LEAVES - 4))

    for d in range(1, NARROW):
        source = pl.ds(pl.multiple_of(lax.rem(n + NARROW - d, NARROW) * SLICE, SLICE), SLICE)
        pltpu.make_async_remote_copy(
            cbuf.at[source], cbuf.at[source], sc.at[d - 1], rc.at[d - 1], device_id=mate(d), device_id_type=MESH
        ).wait_recv()
    node = outv[...] + dot3(split(cbuf[...]), split(ndv[...]), ((1,), (1,)))
    nth_out[...], ntl_out[...] = split(node.T)

    for c in first + second + third + groups + siblings + relays + halo:
        c.wait_send()


def finish(near, mh, ml, nth, ntl, out, buf, sem):
    def done(leaf):
        return pltpu.make_async_copy(buf.at[leaf], out.at[leaf], sem.at[leaf])

    @pl.loop(0, LEAVES)
    def _(leaf):
        buf[leaf] = near[leaf] + dot3((mh[leaf], ml[leaf]), (nth[...], ntl[...]))
        done(leaf).start()

    @pl.loop(0, LEAVES)
    def _(leaf):
        done(leaf).wait()


def shards(cot, rb, cb, lu, nu, nc, gc, nd, ld, nb, ni, fn, fg):
    hbm = pl.BlockSpec(memory_space=pltpu.HBM)
    vmem = pl.BlockSpec(memory_space=pltpu.VMEM)
    dma = pltpu.SemaphoreType.DMA
    shape = jax.ShapeDtypeStruct
    parts = pl.pallas_call(
        exchange,
        out_shape=[
            pltpu.VMEM((LEAVES, PTS, NVEC), F32),
            pltpu.VMEM((LEAVES, PTS, RANK), BF16),
            pltpu.VMEM((LEAVES, PTS, RANK), BF16),
            pltpu.VMEM((RANK, NVEC), BF16),
            pltpu.VMEM((RANK, NVEC), BF16),
        ],
        in_specs=[hbm] * 12 + [pl.BlockSpec(memory_space=pltpu.SMEM)],
        out_specs=[vmem] * 5,
        scratch_shapes=[
            pltpu.VMEM((LEAVES + 2 * REACH, PTS, NVEC), F32),
            pltpu.VMEM((LEAVES, PTS, RANK), F32),
            pltpu.VMEM((LEAVES, PTS, RANK), F32),
            pltpu.VMEM((LEAVES, RANK, RANK), F32),
            pltpu.VMEM((RANK, RANK), F32),
            pltpu.VMEM((2, RANK, RANK), F32),
            pltpu.VMEM((NARROW, RANK + 8, RANK), F32),
            pltpu.VMEM((RANK, RANK), F32),
            pltpu.VMEM((LEAVES, RANK, RANK), F32),
            pltpu.VMEM((LEAVES, NNEAR, PTS, PTS), F32),
            pltpu.VMEM((LEAVES + 2 * REACH, NVEC, PTS), BF16),
            pltpu.VMEM((LEAVES + 2 * REACH, NVEC, PTS), BF16),
            pltpu.VMEM((NVEC, RANK), F32),
            pltpu.VMEM((NARROW, NVEC, RANK), F32),
            pltpu.VMEM((NARROW - 1, SLICE, RANK), F32),
            pltpu.VMEM((WIDE, SLICE, RANK), F32),
            pltpu.VMEM((NVEC, RANK), F32),
            pltpu.VMEM((NVEC, RANK), F32),
            pltpu.SMEM((NNEAR, LEAVES), jnp.int32),
            pltpu.SMEM((1, 2), jnp.int32),
            dma((3, LEAVES)),
            dma((4,)),
            dma((2,)),
            dma((LEAVES,)),
            dma((NARROW - 1,)),
            dma((NARROW - 1,)),
            dma((WIDE - 1,)),
            dma((WIDE - 1,)),
            dma((NARROW - 1,)),
            dma((NARROW - 1,)),
            dma((2 * SIDE - 1,)),
            dma((2 * SIDE - 1,)),
            dma((2 * SIDE - 1,)),
            dma((2 * SIDE - 1,)),
            dma((2,)),
            dma((2,)),
            pltpu.SemaphoreType.REGULAR,
            dma((2,)),
        ],
        compiler_params=pltpu.CompilerParams(
            collective_id=0, has_side_effects=True, vmem_limit_bytes=48 * 2**20
        ),
    )(*[pltpu.with_memory_space_constraint(a, pltpu.HBM) for a in (cot, rb, cb, lu, nu, nc, gc, nd, ld, nb, ni.T, fn)], fg)
    return pl.pallas_call(
        finish,
        out_shape=shape((LEAVES, PTS, NVEC), F32),
        in_specs=[vmem] * 5,
        out_specs=hbm,
        scratch_shapes=[pltpu.VMEM((LEAVES, PTS, NVEC), F32), dma((LEAVES,))],
        compiler_params=pltpu.CompilerParams(vmem_limit_bytes=24 * 2**20),
    )(*parts)


def solution(mesh):
    leaf, both = P(("wide", "narrow"), None, None), P(("wide", "narrow"), None)
    wide4 = P(("wide", "narrow"), None, None, None)
    in_specs = (
        leaf, leaf, leaf, leaf, leaf, wide4, P("wide", "narrow", None, None), leaf, leaf, wide4,
        both, both, P("wide", "narrow"),
    )
    return jax.shard_map(shards, mesh=mesh, in_specs=in_specs, out_specs=leaf, check_vma=False)
```

```python
import functools

import jax
import jax.numpy as jnp
from jax import lax
from jax.experimental import pallas as pl
from jax.experimental.pallas import tpu as pltpu
from jax.sharding import PartitionSpec as P

MESH = pl.DeviceIdType.MESH
F32, BF16 = jnp.float32, jnp.bfloat16
LEAVES, PTS, RANK, NVEC = 12, 256, 128, 256
REACH, NNEAR = 2, 4
PIECES = 4
CHUNK = 3
CHUNKS = LEAVES // CHUNK
AHEAD = 3
PIECE = PTS // PIECES
WIDE, NARROW, SIDE = 16, 8, 4
SLICE = NVEC // NARROW
OFFSETS = [(dz, dx) for dz in (2, 1, 3, 0) for dx in (2, 1, 3, 0) if dz or dx]


def split(value):
    high = value.astype(BF16)
    return high, (value - high.astype(F32)).astype(BF16)


def dot(a, b, dims=((1,), (0,))):
    return lax.dot_general(a, b, (dims, ((), ())), preferred_element_type=F32)


def dot3(a, b, dims=((1,), (0,))):
    (ah, al), (bh, bl) = a, b
    return dot(ah, bh, dims) + (dot(al, bh, dims) + dot(ah, bl, dims))


def exchange(
    cot, rb, cb, lu, nu, nc, gc, nd, ld, nb, ni_hbm, fn_hbm, fg,
    near_out, mm_out, nt_out,
    cotv, rbv, cbv, luv, nuv, ncv, gcv, ndv, ldv, nbv,
    cth, ctl, up_sum, upv, sib, abuf, bbuf, cbuf, outv, ni, fn,
    leaf_sem, small_sem, cb_sem, nb_sem,
    sa, ra, sb, rb_, sc, rc, ss, rs, sg, rg, sh, rh, int_sem,
):
    w, n = lax.axis_index("wide"), lax.axis_index("narrow")
    core = lax.rem(n, 2)

    def mate(d):
        return w, lax.rem(n + d, NARROW)

    def far(dz, dx, sign):
        z = lax.rem(w // SIDE + SIDE + sign * dz, SIDE)
        x = lax.rem(lax.rem(w, SIDE) + SIDE + sign * dx, SIDE)
        return z * SIDE + x, n

    rank = w * NARROW + n
    after, before = lax.rem(rank + 1, WIDE * NARROW), lax.rem(rank + WIDE * NARROW - 1, WIDE * NARROW)
    after, before = (after // NARROW, lax.rem(after, NARROW)), (before // NARROW, lax.rem(before, NARROW))

    barrier = pltpu.get_barrier_semaphore()
    for dz, dx in OFFSETS:
        pl.semaphore_signal(barrier, inc=1, device_id=far(dz, dx, 1), device_id_type=MESH)
    for d in range(1, NARROW):
        pl.semaphore_signal(barrier, inc=1, device_id=mate(d), device_id_type=MESH)
    for to in (after, before):
        pl.semaphore_signal(barrier, inc=1, device_id=to, device_id_type=MESH)

    def chunk_copies(chunk):
        at = pl.ds(chunk * CHUNK, CHUNK)
        return [
            pltpu.make_async_copy(rb.at[at], rbv.at[at], leaf_sem.at[0, chunk]),
            pltpu.make_async_copy(lu.at[at], luv.at[at], leaf_sem.at[1, chunk]),
            pltpu.make_async_copy(cot.at[at], cotv.at[pl.ds(REACH + chunk * CHUNK, CHUNK)], leaf_sem.at[2, chunk]),
        ]

    def near_copy(i):
        leaf = lax.rem(i + REACH, LEAVES)
        return pltpu.make_async_copy(nb.at[leaf], nbv.at[leaf], nb_sem.at[leaf])

    for chunk in range(2):
        for c in chunk_copies(chunk):
            c.start()

    smalls = [
        pltpu.make_async_copy(nu.at[0], nuv, small_sem.at[0]),
        pltpu.make_async_copy(gc.at[0, 0], gcv.at[n, pl.ds(0, RANK)], small_sem.at[1]),
        pltpu.make_async_copy(nc.at[0], ncv, small_sem.at[2]),
        pltpu.make_async_copy(nd.at[0], ndv, small_sem.at[3]),
    ]
    ints = [
        pltpu.make_async_copy(a, b, int_sem.at[i])
        for i, (a, b) in enumerate(((ni_hbm, ni), (fn_hbm, fn)))
    ]
    for c in smalls + ints:
        c.start()
    for c in ints:
        c.wait()

    gcv[n, RANK:, :] = jnp.full((8, RANK), fg[0, 0].astype(F32), F32)
    up_sum[...] = jnp.zeros_like(up_sum)

    def prepare(slot):
        cth[slot], ctl[slot] = split(cotv[slot].T)

    late = [pltpu.make_async_copy(cb, cbv, cb_sem.at[0]), pltpu.make_async_copy(ld, ldv, cb_sem.at[1])]

    @pl.loop(0, CHUNKS)
    def _(chunk):
        for c in chunk_copies(chunk):
            c.wait()

        @pl.when(chunk < CHUNKS - 2)
        def _():
            for c in chunk_copies(chunk + 2):
                c.start()

        @pl.when(chunk == CHUNKS - 2)
        def _():
            for i in range(AHEAD):
                near_copy(i).start()

        @pl.when(chunk == CHUNKS - 1)
        def _():
            for c in late:
                c.start()

        total = None
        for i in range(CHUNK):
            leaf = chunk * CHUNK + i
            lh, ll = split(luv[leaf].T)
            bh, bl = split(rbv[leaf])
            stacked = dot(jnp.concatenate([lh, ll], axis=0), bh, ((1,), (1,)))
            basis = stacked[:RANK] + stacked[RANK:] + dot(lh, bl, ((1,), (1,)))
            bh, bl = split(basis)
            ch, cl = split(cotv[REACH + leaf])
            stacked = dot(jnp.concatenate([bh, bl], axis=0), ch)
            term = stacked[:RANK] + stacked[RANK:] + dot(bh, cl)
            total = term if total is None else total + term
        up_sum[...] += total

    coeffs = up_sum[...].T
    sib[n] = coeffs
    for c in smalls:
        c.wait()
    upv[...] = dot3(split(coeffs), split(nuv[...]))

    pl.semaphore_wait(barrier, len(OFFSETS) + NARROW + 1)

    first = []
    for d in range(1, NARROW):
        to = mate(d)
        first.append(
            pltpu.make_async_remote_copy(
                upv.at[pl.ds(pl.multiple_of(to[1] * SLICE, SLICE), SLICE)], abuf.at[d - 1],
                sa.at[d - 1], ra.at[d - 1], device_id=to, device_id_type=MESH,
            )
        )
        first[-1].start()

    twin = (w, n + 1 - 2 * core)

    def spread(buf, send, recv):
        out = []
        for step in range(SIDE):
            to = twin if step == 0 else mate(2 * step)
            out.append(
                pltpu.make_async_remote_copy(
                    buf.at[n], buf.at[n], send.at[step], recv.at[step], device_id=to, device_id_type=MESH
                )
            )
        return out

    def arrived(buf, send, recv, step):
        source = lax.rem(n + NARROW - 2 * step, NARROW)
        return pltpu.make_async_remote_copy(
            buf.at[source], buf.at[source], send.at[step], recv.at[step], device_id=twin, device_id_type=MESH
        )

    def relay(buf, send, recv, step):
        source = lax.rem(n + NARROW - 2 * step, NARROW)
        return pltpu.make_async_remote_copy(
            buf.at[source], buf.at[source], send.at[SIDE - 1 + step], recv.at[SIDE - 1 + step],
            device_id=twin, device_id_type=MESH,
        )

    groups = spread(gcv, sg, rg)
    siblings = spread(sib, ss, rs)

    def halo(i):
        leaf, rows = i // PIECES, pl.ds(pl.multiple_of(lax.rem(i, PIECES) * PIECE, PIECE), PIECE)
        return [
            pltpu.make_async_remote_copy(
                cot.at[LEAVES - REACH + leaf, rows], cotv.at[leaf, rows],
                sh.at[0, i], rh.at[0, i], device_id=after, device_id_type=MESH,
            ),
            pltpu.make_async_remote_copy(
                cot.at[leaf, rows], cotv.at[REACH + LEAVES + leaf, rows],
                sh.at[1, i], rh.at[1, i], device_id=before, device_id_type=MESH,
            ),
        ]

    def send_halo(low, high):
        @pl.loop(low, high)
        def _(i):
            for c in halo(i):
                c.start()

    def merge_down():
        for c in late:
            c.wait()

        @pl.loop(0, LEAVES, unroll=2)
        def _(leaf):
            wh, wl = split(ldv[leaf])
            row = jnp.concatenate([wh, wl], axis=1)
            both = dot(jnp.concatenate(split(cbv[leaf]), axis=1), jnp.concatenate([row, row], axis=0))
            mm_out[leaf] = jnp.concatenate(split(both[:, :RANK] + both[:, RANK:]), axis=1)

    for c in groups:
        c.start()

    @pl.loop(0, LEAVES, unroll=2)
    def _(leaf):
        prepare(REACH + leaf)

    first_leaf = rank * LEAVES - REACH

    def near(i):
        leaf = lax.rem(i + REACH, LEAVES)
        near_copy(i).wait()

        @pl.when(i + AHEAD < LEAVES)
        def _():
            near_copy(i + AHEAD).start()

        total = None
        for j in range(NNEAR):
            source = jnp.clip(ni[j, leaf] - first_leaf, 0, LEAVES + 2 * REACH - 1)
            term = dot3((cth[source], ctl[source]), split(nbv[leaf, j]))
            total = term if total is None else total + term
        near_out[leaf] = total.T

    @pl.loop(0, 2)
    def _(leaf):
        near(leaf)

    merge_down()

    own = upv[pl.ds(pl.multiple_of(n * SLICE, SLICE), SLICE), :]
    for d, c in enumerate(first):
        c.wait_recv()
        own += abuf[d]
    bbuf[w] = own
    second = []
    for i, (dz, dx) in enumerate(OFFSETS):
        second.append(
            pltpu.make_async_remote_copy(
                bbuf.at[w], bbuf.at[w], sb.at[i], rb_.at[i], device_id=far(dz, dx, 1), device_id_type=MESH
            )
        )
        second[-1].start()

    relays = []
    for step in range(1, SIDE):
        arrived(gcv, sg, rg, step).wait_recv()
        relays.append(relay(gcv, sg, rg, step))
        relays[-1].start()

    send_halo(0, 8)

    for c in siblings:
        c.start()

    @pl.loop(2, 8)
    def _(leaf):
        near(leaf)

    for step in range(1, SIDE):
        arrived(sib, ss, rs, step).wait_recv()
        relays.append(relay(sib, ss, rs, step))
        relays[-1].start()

    def from_twin(buf, send, recv, step):
        at = 0 if step == 0 else SIDE - 1 + step
        source = lax.rem(twin[1] + NARROW - 2 * step, NARROW)
        return pltpu.make_async_remote_copy(
            buf.at[source], buf.at[source], send.at[at], recv.at[at], device_id=twin, device_id_type=MESH
        )

    for step in range(SIDE):
        from_twin(gcv, sg, rg, step).wait_recv()
    for i, (dz, dx) in enumerate(OFFSETS):
        source = far(dz, dx, -1)[0]
        pltpu.make_async_remote_copy(
            bbuf.at[source], bbuf.at[source], sb.at[i], rb_.at[i], device_id=far(dz, dx, 1), device_id_type=MESH
        ).wait_recv()

    part = jnp.zeros((SLICE, RANK), F32)
    for j in range(NARROW):
        tag = jnp.concatenate([gcv[j, RANK:, :]] * (SLICE // 8), axis=0)
        picked = bbuf[0]
        for g in range(1, WIDE):
            picked = jnp.where(tag == float(g), bbuf[g], picked)
        part += dot3(split(picked), split(gcv[j, :RANK, :]))
    mine = pl.ds(pl.multiple_of(n * SLICE, SLICE), SLICE)
    cbuf[mine, :] = part
    third = []
    for d in range(1, NARROW):
        third.append(
            pltpu.make_async_remote_copy(
                cbuf.at[mine], cbuf.at[mine], sc.at[d - 1], rc.at[d - 1], device_id=mate(d), device_id_type=MESH
            )
        )
        third[-1].start()

    for step in range(SIDE):
        from_twin(sib, ss, rs, step).wait_recv()
    node = jnp.zeros((NVEC, RANK), F32)
    for j in range(2):
        node += dot3(split(sib[jnp.clip(fn[0, j], 0, NARROW - 1)]), split(ncv[j]))
    outv[...] = node

    @pl.loop(0, REACH * PIECES)
    def _(i):
        for c in halo(i):
            c.wait_recv()

    for slot in (0, 1, REACH + LEAVES, REACH + LEAVES + 1):
        prepare(slot)

    @pl.loop(LEAVES - 2 * REACH, LEAVES)
    def _(i):
        near(i)

    for d in range(1, NARROW):
        source = pl.ds(pl.multiple_of(lax.rem(n + NARROW - d, NARROW) * SLICE, SLICE), SLICE)
        pltpu.make_async_remote_copy(
            cbuf.at[source], cbuf.at[source], sc.at[d - 1], rc.at[d - 1], device_id=mate(d), device_id_type=MESH
        ).wait_recv()
    node = outv[...] + dot3(split(cbuf[...]), split(ndv[...]), ((1,), (1,)))
    high, low = split(node.T)
    nt_out[0:RANK], nt_out[RANK : 2 * RANK], nt_out[2 * RANK :] = high, high, low

    for c in first + second + third + groups + siblings + relays:
        c.wait_send()

    @pl.loop(0, REACH * PIECES)
    def _(i):
        for c in halo(i):
            c.wait_send()


def finish(near, mm, nt, out, buf, sem):
    def done(leaf):
        return pltpu.make_async_copy(buf.at[leaf], out.at[leaf], sem.at[leaf])

    @pl.loop(0, LEAVES, unroll=2)
    def _(leaf):
        far = dot(mm[leaf], nt[: 2 * RANK]) + dot(mm[leaf, :, :RANK], nt[2 * RANK :])
        buf[leaf] = near[leaf] + far
        done(leaf).start()

    @pl.loop(0, LEAVES)
    def _(leaf):
        done(leaf).wait()


def shards(cot, rb, cb, lu, nu, nc, gc, nd, ld, nb, ni, fn, fg):
    hbm = pl.BlockSpec(memory_space=pltpu.HBM)
    vmem = pl.BlockSpec(memory_space=pltpu.VMEM)
    dma = pltpu.SemaphoreType.DMA
    shape = jax.ShapeDtypeStruct
    parts = pl.pallas_call(
        exchange,
        out_shape=[
            pltpu.VMEM((LEAVES, PTS, NVEC), F32),
            pltpu.VMEM((LEAVES, PTS, 2 * RANK), BF16),
            pltpu.VMEM((3 * RANK, NVEC), BF16),
        ],
        in_specs=[hbm] * 12 + [pl.BlockSpec(memory_space=pltpu.SMEM)],
        out_specs=[vmem] * 3,
        scratch_shapes=[
            pltpu.VMEM((LEAVES + 2 * REACH, PTS, NVEC), F32),
            pltpu.VMEM((LEAVES, PTS, RANK), F32),
            pltpu.VMEM((LEAVES, PTS, RANK), F32),
            pltpu.VMEM((LEAVES, RANK, RANK), F32),
            pltpu.VMEM((RANK, RANK), F32),
            pltpu.VMEM((2, RANK, RANK), F32),
            pltpu.VMEM((NARROW, RANK + 8, RANK), F32),
            pltpu.VMEM((RANK, RANK), F32),
            pltpu.VMEM((LEAVES, RANK, RANK), F32),
            pltpu.VMEM((LEAVES, NNEAR, PTS, PTS), F32),
            pltpu.VMEM((LEAVES + 2 * REACH, NVEC, PTS), BF16),
            pltpu.VMEM((LEAVES + 2 * REACH, NVEC, PTS), BF16),
            pltpu.VMEM((RANK, NVEC), F32),
            pltpu.VMEM((NVEC, RANK), F32),
            pltpu.VMEM((NARROW, NVEC, RANK), F32),
            pltpu.VMEM((NARROW - 1, SLICE, RANK), F32),
            pltpu.VMEM((WIDE, SLICE, RANK), F32),
            pltpu.VMEM((NVEC, RANK), F32),
            pltpu.VMEM((NVEC, RANK), F32),
            pltpu.SMEM((NNEAR, LEAVES), jnp.int32),
            pltpu.SMEM((1, 2), jnp.int32),
            dma((3, CHUNKS)),
            dma((4,)),
            dma((2,)),
            dma((LEAVES,)),
            dma((NARROW - 1,)),
            dma((NARROW - 1,)),
            dma((WIDE - 1,)),
            dma((WIDE - 1,)),
            dma((NARROW - 1,)),
            dma((NARROW - 1,)),
            dma((2 * SIDE - 1,)),
            dma((2 * SIDE - 1,)),
            dma((2 * SIDE - 1,)),
            dma((2 * SIDE - 1,)),
            dma((2, REACH * PIECES)),
            dma((2, REACH * PIECES)),
            dma((2,)),
        ],
        compiler_params=pltpu.CompilerParams(
            collective_id=0, has_side_effects=True, vmem_limit_bytes=48 * 2**20
        ),
    )(*[pltpu.with_memory_space_constraint(a, pltpu.HBM) for a in (cot, rb, cb, lu, nu, nc, gc, nd, ld, nb, ni.T, fn)], fg)
    return pl.pallas_call(
        finish,
        out_shape=shape((LEAVES, PTS, NVEC), F32),
        in_specs=[vmem] * 3,
        out_specs=hbm,
        scratch_shapes=[pltpu.VMEM((LEAVES, PTS, NVEC), F32), dma((LEAVES,))],
        compiler_params=pltpu.CompilerParams(vmem_limit_bytes=24 * 2**20),
    )(*parts)


def solution(mesh):
    leaf, both = P(("wide", "narrow"), None, None), P(("wide", "narrow"), None)
    wide4 = P(("wide", "narrow"), None, None, None)
    in_specs = (
        leaf, leaf, leaf, leaf, leaf, wide4, P("wide", "narrow", None, None), leaf, leaf, wide4,
        both, both, P("wide", "narrow"),
    )
    return jax.shard_map(shards, mesh=mesh, in_specs=in_specs, out_specs=leaf, check_vma=False)
```

```python
import functools

import jax
import jax.numpy as jnp
from jax import lax
from jax.experimental import pallas as pl
from jax.experimental.pallas import tpu as pltpu
from jax.sharding import PartitionSpec as P

MESH = pl.DeviceIdType.MESH
F32, BF16 = jnp.float32, jnp.bfloat16
LEAVES, PTS, RANK, NVEC = 12, 256, 128, 256
REACH, NNEAR = 2, 4
PIECES = 1
CHUNK = 6
CHUNKS = LEAVES // CHUNK
AHEAD = 3
PIECE = PTS // PIECES
WIDE, NARROW, SIDE = 16, 8, 4
SLICE = NVEC // NARROW
OFFSETS = [(dz, dx) for dz in (2, 1, 3, 0) for dx in (2, 1, 3, 0) if dz or dx]


def split(value):
    high = value.astype(BF16)
    return high, (value - high.astype(F32)).astype(BF16)


def dot(a, b, dims=((1,), (0,))):
    return lax.dot_general(a, b, (dims, ((), ())), preferred_element_type=F32)


def dot3(a, b, dims=((1,), (0,))):
    (ah, al), (bh, bl) = a, b
    return dot(ah, bh, dims) + (dot(al, bh, dims) + dot(ah, bl, dims))


def exchange(
    cot, rb, cb, lu, nu, nc, gc, nd, ld, nb, ni_hbm, fn_hbm, fg,
    near_out, mm_out, nt_out,
    cotv, rbv, cbv, luv, nuv, ncv, gcv, ndv, ldv, nbv,
    cth, ctl, up_sum, upv, sib, abuf, bbuf, cbuf, outv, gch, gcl, ni, fn,
    leaf_sem, small_sem, cb_sem, nb_sem,
    sa, ra, sb, rb_, sc, rc, ss, rs, sg, rg, sh, rh, int_sem,
):
    w, n = lax.axis_index("wide"), lax.axis_index("narrow")
    core = lax.rem(n, 2)

    def mate(d):
        return w, lax.rem(n + d, NARROW)

    def far(dz, dx, sign):
        z = lax.rem(w // SIDE + SIDE + sign * dz, SIDE)
        x = lax.rem(lax.rem(w, SIDE) + SIDE + sign * dx, SIDE)
        return z * SIDE + x, n

    rank = w * NARROW + n
    after, before = lax.rem(rank + 1, WIDE * NARROW), lax.rem(rank + WIDE * NARROW - 1, WIDE * NARROW)
    after, before = (after // NARROW, lax.rem(after, NARROW)), (before // NARROW, lax.rem(before, NARROW))

    barrier = pltpu.get_barrier_semaphore()
    for dz, dx in OFFSETS:
        pl.semaphore_signal(barrier, inc=1, device_id=far(dz, dx, 1), device_id_type=MESH)
    for d in range(1, NARROW):
        pl.semaphore_signal(barrier, inc=1, device_id=mate(d), device_id_type=MESH)
    for to in (after, before):
        pl.semaphore_signal(barrier, inc=1, device_id=to, device_id_type=MESH)

    def chunk_copies(chunk):
        at = pl.ds(chunk * CHUNK, CHUNK)
        return [
            pltpu.make_async_copy(rb.at[at], rbv.at[at], leaf_sem.at[0, chunk]),
            pltpu.make_async_copy(lu.at[at], luv.at[at], leaf_sem.at[1, chunk]),
            pltpu.make_async_copy(cot.at[at], cotv.at[pl.ds(REACH + chunk * CHUNK, CHUNK)], leaf_sem.at[2, chunk]),
        ]

    def near_copy(i):
        leaf = lax.rem(i + REACH, LEAVES)
        return pltpu.make_async_copy(nb.at[leaf], nbv.at[leaf], nb_sem.at[leaf])

    for chunk in range(2):
        for c in chunk_copies(chunk):
            c.start()

    smalls = [
        pltpu.make_async_copy(nu.at[0], nuv, small_sem.at[0]),
        pltpu.make_async_copy(gc.at[0, 0], gcv.at[n, pl.ds(0, RANK)], small_sem.at[1]),
        pltpu.make_async_copy(nc.at[0], ncv, small_sem.at[2]),
        pltpu.make_async_copy(nd.at[0], ndv, small_sem.at[3]),
    ]
    ints = [
        pltpu.make_async_copy(a, b, int_sem.at[i])
        for i, (a, b) in enumerate(((ni_hbm, ni), (fn_hbm, fn)))
    ]
    for c in smalls + ints:
        c.start()
    for c in ints:
        c.wait()

    gcv[n, RANK:, :] = jnp.full((8, RANK), fg[0, 0].astype(F32), F32)
    up_sum[...] = jnp.zeros_like(up_sum)

    def prepare(slot):
        cth[slot], ctl[slot] = split(cotv[slot].T)

    late = [pltpu.make_async_copy(cb, cbv, cb_sem.at[0]), pltpu.make_async_copy(ld, ldv, cb_sem.at[1])]

    @pl.loop(0, CHUNKS)
    def _(chunk):
        for c in chunk_copies(chunk):
            c.wait()

        @pl.when(chunk < CHUNKS - 2)
        def _():
            for c in chunk_copies(chunk + 2):
                c.start()

        @pl.when(chunk == CHUNKS - 2)
        def _():
            for i in range(AHEAD):
                near_copy(i).start()

        @pl.when(chunk == CHUNKS - 1)
        def _():
            for c in late:
                c.start()

        total = None
        for i in range(CHUNK):
            leaf = chunk * CHUNK + i
            lh, ll = split(luv[leaf].T)
            bh, bl = split(rbv[leaf])
            stacked = dot(jnp.concatenate([lh, ll], axis=0), bh, ((1,), (1,)))
            basis = stacked[:RANK] + stacked[RANK:] + dot(lh, bl, ((1,), (1,)))
            bh, bl = split(basis)
            ch, cl = split(cotv[REACH + leaf])
            stacked = dot(jnp.concatenate([bh, bl], axis=0), ch)
            term = stacked[:RANK] + stacked[RANK:] + dot(bh, cl)
            total = term if total is None else total + term
        up_sum[...] += total

    coeffs = up_sum[...].T
    sib[n] = coeffs
    for c in smalls:
        c.wait()
    upv[...] = dot3(split(coeffs), split(nuv[...]))

    pl.semaphore_wait(barrier, len(OFFSETS) + NARROW + 1)

    first = []
    for d in range(1, NARROW):
        to = mate(d)
        first.append(
            pltpu.make_async_remote_copy(
                upv.at[pl.ds(pl.multiple_of(to[1] * SLICE, SLICE), SLICE)], abuf.at[d - 1],
                sa.at[d - 1], ra.at[d - 1], device_id=to, device_id_type=MESH,
            )
        )
        first[-1].start()

    twin = (w, n + 1 - 2 * core)

    def spread(buf, send, recv):
        out = []
        for step in range(SIDE):
            to = twin if step == 0 else mate(2 * step)
            out.append(
                pltpu.make_async_remote_copy(
                    buf.at[n], buf.at[n], send.at[step], recv.at[step], device_id=to, device_id_type=MESH
                )
            )
        return out

    def arrived(buf, send, recv, step):
        source = lax.rem(n + NARROW - 2 * step, NARROW)
        return pltpu.make_async_remote_copy(
            buf.at[source], buf.at[source], send.at[step], recv.at[step], device_id=twin, device_id_type=MESH
        )

    def relay(buf, send, recv, step):
        source = lax.rem(n + NARROW - 2 * step, NARROW)
        return pltpu.make_async_remote_copy(
            buf.at[source], buf.at[source], send.at[SIDE - 1 + step], recv.at[SIDE - 1 + step],
            device_id=twin, device_id_type=MESH,
        )

    groups = spread(gcv, sg, rg)
    siblings = spread(sib, ss, rs)

    def halo(i):
        leaf, rows = i // PIECES, pl.ds(pl.multiple_of(lax.rem(i, PIECES) * PIECE, PIECE), PIECE)
        return [
            pltpu.make_async_remote_copy(
                cot.at[LEAVES - REACH + leaf, rows], cotv.at[leaf, rows],
                sh.at[0, i], rh.at[0, i], device_id=after, device_id_type=MESH,
            ),
            pltpu.make_async_remote_copy(
                cot.at[leaf, rows], cotv.at[REACH + LEAVES + leaf, rows],
                sh.at[1, i], rh.at[1, i], device_id=before, device_id_type=MESH,
            ),
        ]

    def send_halo(low, high):
        @pl.loop(low, high)
        def _(i):
            for c in halo(i):
                c.start()

    def merge_down():
        for c in late:
            c.wait()

        @pl.loop(0, LEAVES, unroll=2)
        def _(leaf):
            wh, wl = split(ldv[leaf])
            row = jnp.concatenate([wh, wl], axis=1)
            both = dot(jnp.concatenate(split(cbv[leaf]), axis=1), jnp.concatenate([row, row], axis=0))
            mm_out[leaf] = jnp.concatenate(split(both[:, :RANK] + both[:, RANK:]), axis=1)

    for c in groups:
        c.start()

    send_halo(0, 2)

    @pl.loop(0, LEAVES, unroll=2)
    def _(leaf):
        prepare(REACH + leaf)

    first_leaf = rank * LEAVES - REACH

    def near(i):
        leaf = lax.rem(i + REACH, LEAVES)
        near_copy(i).wait()

        @pl.when(i + AHEAD < LEAVES)
        def _():
            near_copy(i + AHEAD).start()

        total = None
        for j in range(NNEAR):
            source = jnp.clip(ni[j, leaf] - first_leaf, 0, LEAVES + 2 * REACH - 1)
            term = dot3((cth[source], ctl[source]), split(nbv[leaf, j]))
            total = term if total is None else total + term
        near_out[leaf] = total.T

    @pl.loop(0, 2)
    def _(leaf):
        near(leaf)

    merge_down()

    own = upv[pl.ds(pl.multiple_of(n * SLICE, SLICE), SLICE), :]
    for d, c in enumerate(first):
        c.wait_recv()
        own += abuf[d]
    bbuf[w] = own
    second = []
    for i, (dz, dx) in enumerate(OFFSETS):
        second.append(
            pltpu.make_async_remote_copy(
                bbuf.at[w], bbuf.at[w], sb.at[i], rb_.at[i], device_id=far(dz, dx, 1), device_id_type=MESH
            )
        )
        second[-1].start()

    relays = []

    def pass_on(*steps):
        for step in steps:
            arrived(sib, ss, rs, step).wait_recv()
            relays.append(relay(sib, ss, rs, step))
            relays[-1].start()

    for step in range(1, SIDE):
        arrived(gcv, sg, rg, step).wait_recv()
        relays.append(relay(gcv, sg, rg, step))
        relays[-1].start()

    for c in siblings:
        c.start()

    @pl.loop(2, 8)
    def _(leaf):
        near(leaf)

    def from_twin(buf, send, recv, step):
        at = 0 if step == 0 else SIDE - 1 + step
        source = lax.rem(twin[1] + NARROW - 2 * step, NARROW)
        return pltpu.make_async_remote_copy(
            buf.at[source], buf.at[source], send.at[at], recv.at[at], device_id=twin, device_id_type=MESH
        )

    for step in range(SIDE):
        from_twin(gcv, sg, rg, step).wait_recv()

    @pl.loop(0, NARROW)
    def _(j):
        rows = pl.ds(pl.multiple_of(j * RANK, RANK), RANK)
        gch[rows, :], gcl[rows, :] = split(gcv[j, :RANK, :])

    for i, (dz, dx) in enumerate(OFFSETS):
        source = far(dz, dx, -1)[0]
        pltpu.make_async_remote_copy(
            bbuf.at[source], bbuf.at[source], sb.at[i], rb_.at[i], device_id=far(dz, dx, 1), device_id_type=MESH
        ).wait_recv()

    picked = []
    for j in range(NARROW):
        tag = jnp.concatenate([gcv[j, RANK:, :]] * (SLICE // 8), axis=0)
        value = bbuf[0]
        for g in range(1, WIDE):
            value = jnp.where(tag == float(g), bbuf[g], value)
        picked.append(value)
    high, low = split(jnp.concatenate(picked, axis=1))
    both = dot(jnp.concatenate([high, low], axis=0), gch[...])
    part = both[:SLICE] + both[SLICE:] + dot(high, gcl[...])
    mine = pl.ds(pl.multiple_of(n * SLICE, SLICE), SLICE)
    cbuf[mine, :] = part
    third = []
    for d in range(1, NARROW):
        third.append(
            pltpu.make_async_remote_copy(
                cbuf.at[mine], cbuf.at[mine], sc.at[d - 1], rc.at[d - 1], device_id=mate(d), device_id_type=MESH
            )
        )
        third[-1].start()

    @pl.loop(0, REACH * PIECES)
    def _(i):
        for c in halo(i):
            c.wait_recv()

    for slot in (0, 1, REACH + LEAVES, REACH + LEAVES + 1):
        prepare(slot)

    @pl.loop(LEAVES - 2 * REACH, LEAVES)
    def _(i):
        near(i)

    pass_on(1, 2, 3)

    for step in range(SIDE):
        from_twin(sib, ss, rs, step).wait_recv()
    node = jnp.zeros((NVEC, RANK), F32)
    for j in range(2):
        node += dot3(split(sib[jnp.clip(fn[0, j], 0, NARROW - 1)]), split(ncv[j]))
    outv[...] = node

    for d in range(1, NARROW):
        source = pl.ds(pl.multiple_of(lax.rem(n + NARROW - d, NARROW) * SLICE, SLICE), SLICE)
        pltpu.make_async_remote_copy(
            cbuf.at[source], cbuf.at[source], sc.at[d - 1], rc.at[d - 1], device_id=mate(d), device_id_type=MESH
        ).wait_recv()
    node = outv[...] + dot3(split(cbuf[...]), split(ndv[...]), ((1,), (1,)))
    high, low = split(node.T)
    nt_out[0:RANK], nt_out[RANK : 2 * RANK], nt_out[2 * RANK :] = high, high, low

    for c in first + second + third + groups + siblings + relays:
        c.wait_send()

    @pl.loop(0, REACH * PIECES)
    def _(i):
        for c in halo(i):
            c.wait_send()


def finish(near, mm, nt, out, buf, sem):
    def done(leaf):
        return pltpu.make_async_copy(buf.at[leaf], out.at[leaf], sem.at[leaf])

    @pl.loop(0, LEAVES, unroll=6)
    def _(leaf):
        far = dot(mm[leaf], nt[: 2 * RANK]) + dot(mm[leaf, :, :RANK], nt[2 * RANK :])
        buf[leaf] = near[leaf] + far
        done(leaf).start()

    @pl.loop(0, LEAVES)
    def _(leaf):
        done(leaf).wait()


def shards(cot, rb, cb, lu, nu, nc, gc, nd, ld, nb, ni, fn, fg):
    hbm = pl.BlockSpec(memory_space=pltpu.HBM)
    vmem = pl.BlockSpec(memory_space=pltpu.VMEM)
    dma = pltpu.SemaphoreType.DMA
    shape = jax.ShapeDtypeStruct
    parts = pl.pallas_call(
        exchange,
        out_shape=[
            pltpu.VMEM((LEAVES, PTS, NVEC), F32),
            pltpu.VMEM((LEAVES, PTS, 2 * RANK), BF16),
            pltpu.VMEM((3 * RANK, NVEC), BF16),
        ],
        in_specs=[hbm] * 12 + [pl.BlockSpec(memory_space=pltpu.SMEM)],
        out_specs=[vmem] * 3,
        scratch_shapes=[
            pltpu.VMEM((LEAVES + 2 * REACH, PTS, NVEC), F32),
            pltpu.VMEM((LEAVES, PTS, RANK), F32),
            pltpu.VMEM((LEAVES, PTS, RANK), F32),
            pltpu.VMEM((LEAVES, RANK, RANK), F32),
            pltpu.VMEM((RANK, RANK), F32),
            pltpu.VMEM((2, RANK, RANK), F32),
            pltpu.VMEM((NARROW, RANK + 8, RANK), F32),
            pltpu.VMEM((RANK, RANK), F32),
            pltpu.VMEM((LEAVES, RANK, RANK), F32),
            pltpu.VMEM((LEAVES, NNEAR, PTS, PTS), F32),
            pltpu.VMEM((LEAVES + 2 * REACH, NVEC, PTS), BF16),
            pltpu.VMEM((LEAVES + 2 * REACH, NVEC, PTS), BF16),
            pltpu.VMEM((RANK, NVEC), F32),
            pltpu.VMEM((NVEC, RANK), F32),
            pltpu.VMEM((NARROW, NVEC, RANK), F32),
            pltpu.VMEM((NARROW - 1, SLICE, RANK), F32),
            pltpu.VMEM((WIDE, SLICE, RANK), F32),
            pltpu.VMEM((NVEC, RANK), F32),
            pltpu.VMEM((NVEC, RANK), F32),
            pltpu.VMEM((NARROW * RANK, RANK), BF16),
            pltpu.VMEM((NARROW * RANK, RANK), BF16),
            pltpu.SMEM((NNEAR, LEAVES), jnp.int32),
            pltpu.SMEM((1, 2), jnp.int32),
            dma((3, CHUNKS)),
            dma((4,)),
            dma((2,)),
            dma((LEAVES,)),
            dma((NARROW - 1,)),
            dma((NARROW - 1,)),
            dma((WIDE - 1,)),
            dma((WIDE - 1,)),
            dma((NARROW - 1,)),
            dma((NARROW - 1,)),
            dma((2 * SIDE - 1,)),
            dma((2 * SIDE - 1,)),
            dma((2 * SIDE - 1,)),
            dma((2 * SIDE - 1,)),
            dma((2, REACH * PIECES)),
            dma((2, REACH * PIECES)),
            dma((2,)),
        ],
        compiler_params=pltpu.CompilerParams(
            collective_id=0, has_side_effects=True, vmem_limit_bytes=48 * 2**20
        ),
    )(*[pltpu.with_memory_space_constraint(a, pltpu.HBM) for a in (cot, rb, cb, lu, nu, nc, gc, nd, ld, nb, ni.T, fn)], fg)
    return pl.pallas_call(
        finish,
        out_shape=shape((LEAVES, PTS, NVEC), F32),
        in_specs=[vmem] * 3,
        out_specs=hbm,
        scratch_shapes=[pltpu.VMEM((LEAVES, PTS, NVEC), F32), dma((LEAVES,))],
        compiler_params=pltpu.CompilerParams(vmem_limit_bytes=24 * 2**20),
    )(*parts)


def solution(mesh):
    leaf, both = P(("wide", "narrow"), None, None), P(("wide", "narrow"), None)
    wide4 = P(("wide", "narrow"), None, None, None)
    in_specs = (
        leaf, leaf, leaf, leaf, leaf, wide4, P("wide", "narrow", None, None), leaf, leaf, wide4,
        both, both, P("wide", "narrow"),
    )
    return jax.shard_map(shards, mesh=mesh, in_specs=in_specs, out_specs=leaf, check_vma=False)
```

```python
import functools

import jax
import jax.numpy as jnp
from jax import lax
from jax.experimental import pallas as pl
from jax.experimental.pallas import tpu as pltpu
from jax.sharding import PartitionSpec as P

MESH = pl.DeviceIdType.MESH
F32, BF16 = jnp.float32, jnp.bfloat16
LEAVES, PTS, RANK, NVEC = 12, 256, 128, 256
REACH, NNEAR = 2, 4
PIECES = 1
CHUNK = 6
CHUNKS = LEAVES // CHUNK
AHEAD = 3
PIECE = PTS // PIECES
WIDE, NARROW, SIDE = 16, 8, 4
SLICE = NVEC // NARROW
OFFSETS = [(dz, dx) for dz in (2, 1, 3, 0) for dx in (2, 1, 3, 0) if dz or dx]


def split(value):
    high = value.astype(BF16)
    return high, (value - high.astype(F32)).astype(BF16)


def dot(a, b, dims=((1,), (0,))):
    return lax.dot_general(a, b, (dims, ((), ())), preferred_element_type=F32)


def dot3(a, b, dims=((1,), (0,))):
    (ah, al), (bh, bl) = a, b
    return dot(ah, bh, dims) + (dot(al, bh, dims) + dot(ah, bl, dims))


def exchange(
    cot, rb, cb, lu, nu, nc, gc, nd, ld, nb, ni_hbm, fn_hbm, fg,
    near_out, mm_out, nt_out,
    cotv, rbv, cbv, luv, nuv, ncv, gcv, ndv, ldv, nbv,
    cth, ctl, up_sum, upv, sib, abuf, bbuf, cbuf, outv, gch, gcl, ni, fn,
    leaf_sem, small_sem, cb_sem, nb_sem,
    sa, ra, sb, rb_, sc, rc, ss, rs, sg, rg, sh, rh, int_sem,
):
    w, n = lax.axis_index("wide"), lax.axis_index("narrow")
    core = lax.rem(n, 2)

    def mate(d):
        return w, lax.rem(n + d, NARROW)

    def far(dz, dx, sign):
        z = lax.rem(w // SIDE + SIDE + sign * dz, SIDE)
        x = lax.rem(lax.rem(w, SIDE) + SIDE + sign * dx, SIDE)
        return z * SIDE + x, n

    rank = w * NARROW + n
    after, before = lax.rem(rank + 1, WIDE * NARROW), lax.rem(rank + WIDE * NARROW - 1, WIDE * NARROW)
    after, before = (after // NARROW, lax.rem(after, NARROW)), (before // NARROW, lax.rem(before, NARROW))

    barrier = pltpu.get_barrier_semaphore()
    for dz, dx in OFFSETS:
        pl.semaphore_signal(barrier, inc=1, device_id=far(dz, dx, 1), device_id_type=MESH)
    for d in range(1, NARROW):
        pl.semaphore_signal(barrier, inc=1, device_id=mate(d), device_id_type=MESH)
    for to in (after, before):
        pl.semaphore_signal(barrier, inc=1, device_id=to, device_id_type=MESH)

    def chunk_copies(chunk):
        at = pl.ds(chunk * CHUNK, CHUNK)
        return [
            pltpu.make_async_copy(rb.at[at], rbv.at[at], leaf_sem.at[0, chunk]),
            pltpu.make_async_copy(lu.at[at], luv.at[at], leaf_sem.at[1, chunk]),
            pltpu.make_async_copy(cot.at[at], cotv.at[pl.ds(REACH + chunk * CHUNK, CHUNK)], leaf_sem.at[2, chunk]),
        ]

    def near_copy(i):
        leaf = lax.rem(i + REACH, LEAVES)
        return pltpu.make_async_copy(nb.at[leaf], nbv.at[leaf], nb_sem.at[leaf])

    for chunk in range(2):
        for c in chunk_copies(chunk):
            c.start()

    smalls = [
        pltpu.make_async_copy(nu.at[0], nuv, small_sem.at[0]),
        pltpu.make_async_copy(gc.at[0, 0], gcv.at[n, pl.ds(0, RANK)], small_sem.at[1]),
        pltpu.make_async_copy(nc.at[0], ncv, small_sem.at[2]),
        pltpu.make_async_copy(nd.at[0], ndv, small_sem.at[3]),
    ]
    ints = [
        pltpu.make_async_copy(a, b, int_sem.at[i])
        for i, (a, b) in enumerate(((ni_hbm, ni), (fn_hbm, fn)))
    ]
    for c in smalls + ints:
        c.start()
    for c in ints:
        c.wait()

    gcv[n, RANK:, :] = jnp.full((8, RANK), fg[0, 0].astype(F32), F32)
    up_sum[...] = jnp.zeros_like(up_sum)

    def prepare(slot):
        cth[slot], ctl[slot] = split(cotv[slot].T)

    late = [pltpu.make_async_copy(cb, cbv, cb_sem.at[0]), pltpu.make_async_copy(ld, ldv, cb_sem.at[1])]

    @pl.loop(0, CHUNKS)
    def _(chunk):
        for c in chunk_copies(chunk):
            c.wait()

        @pl.when(chunk < CHUNKS - 2)
        def _():
            for c in chunk_copies(chunk + 2):
                c.start()

        @pl.when(chunk == CHUNKS - 2)
        def _():
            for i in range(AHEAD):
                near_copy(i).start()

        @pl.when(chunk == CHUNKS - 1)
        def _():
            for c in late:
                c.start()

        total = None
        for i in range(CHUNK):
            leaf = chunk * CHUNK + i
            lh, ll = split(luv[leaf].T)
            bh, bl = split(rbv[leaf])
            stacked = dot(jnp.concatenate([lh, ll], axis=0), bh, ((1,), (1,)))
            basis = stacked[:RANK] + stacked[RANK:] + dot(lh, bl, ((1,), (1,)))
            bh, bl = split(basis)
            ch, cl = split(cotv[REACH + leaf])
            stacked = dot(jnp.concatenate([bh, bl], axis=0), ch)
            term = stacked[:RANK] + stacked[RANK:] + dot(bh, cl)
            total = term if total is None else total + term
        up_sum[...] += total

    coeffs = up_sum[...].T
    sib[n] = coeffs
    for c in smalls:
        c.wait()
    upv[...] = dot3(split(coeffs), split(nuv[...]))

    pl.semaphore_wait(barrier, len(OFFSETS) + NARROW + 1)

    first = []
    for d in range(1, NARROW):
        to = mate(d)
        first.append(
            pltpu.make_async_remote_copy(
                upv.at[pl.ds(pl.multiple_of(to[1] * SLICE, SLICE), SLICE)], abuf.at[d - 1],
                sa.at[d - 1], ra.at[d - 1], device_id=to, device_id_type=MESH,
            )
        )
        first[-1].start()

    twin = (w, n + 1 - 2 * core)

    def spread(buf, send, recv):
        out = []
        for step in range(SIDE):
            to = twin if step == 0 else mate(2 * step)
            out.append(
                pltpu.make_async_remote_copy(
                    buf.at[n], buf.at[n], send.at[step], recv.at[step], device_id=to, device_id_type=MESH
                )
            )
        return out

    def arrived(buf, send, recv, step):
        source = lax.rem(n + NARROW - 2 * step, NARROW)
        return pltpu.make_async_remote_copy(
            buf.at[source], buf.at[source], send.at[step], recv.at[step], device_id=twin, device_id_type=MESH
        )

    def relay(buf, send, recv, step):
        source = lax.rem(n + NARROW - 2 * step, NARROW)
        return pltpu.make_async_remote_copy(
            buf.at[source], buf.at[source], send.at[SIDE - 1 + step], recv.at[SIDE - 1 + step],
            device_id=twin, device_id_type=MESH,
        )

    groups = spread(gcv, sg, rg)
    siblings = spread(sib, ss, rs)

    def halo(i):
        leaf, rows = i // PIECES, pl.ds(pl.multiple_of(lax.rem(i, PIECES) * PIECE, PIECE), PIECE)
        return [
            pltpu.make_async_remote_copy(
                cot.at[LEAVES - REACH + leaf, rows], cotv.at[leaf, rows],
                sh.at[0, i], rh.at[0, i], device_id=after, device_id_type=MESH,
            ),
            pltpu.make_async_remote_copy(
                cot.at[leaf, rows], cotv.at[REACH + LEAVES + leaf, rows],
                sh.at[1, i], rh.at[1, i], device_id=before, device_id_type=MESH,
            ),
        ]

    def send_halo(low, high):
        @pl.loop(low, high)
        def _(i):
            for c in halo(i):
                c.start()

    def merge_down():
        for c in late:
            c.wait()

        @pl.loop(0, LEAVES, unroll=2)
        def _(leaf):
            wh, wl = split(ldv[leaf])
            row = jnp.concatenate([wh, wl], axis=1)
            both = dot(jnp.concatenate(split(cbv[leaf]), axis=1), jnp.concatenate([row, row], axis=0))
            mm_out[leaf] = jnp.concatenate(split(both[:, :RANK] + both[:, RANK:]), axis=1)

    send_halo(0, 2)

    for c in groups:
        c.start()

    @pl.loop(0, LEAVES, unroll=2)
    def _(leaf):
        prepare(REACH + leaf)

    first_leaf = rank * LEAVES - REACH

    def near(i):
        leaf = lax.rem(i + REACH, LEAVES)
        near_copy(i).wait()

        @pl.when(i + AHEAD < LEAVES)
        def _():
            near_copy(i + AHEAD).start()

        total = None
        for j in range(NNEAR):
            source = jnp.clip(ni[j, leaf] - first_leaf, 0, LEAVES + 2 * REACH - 1)
            term = dot3((cth[source], ctl[source]), split(nbv[leaf, j]))
            total = term if total is None else total + term
        near_out[leaf] = total.T

    @pl.loop(0, 2)
    def _(leaf):
        near(leaf)

    merge_down()

    own = upv[pl.ds(pl.multiple_of(n * SLICE, SLICE), SLICE), :]
    for d, c in enumerate(first):
        c.wait_recv()
        own += abuf[d]
    bbuf[w] = own
    second = []
    for i, (dz, dx) in enumerate(OFFSETS):
        second.append(
            pltpu.make_async_remote_copy(
                bbuf.at[w], bbuf.at[w], sb.at[i], rb_.at[i], device_id=far(dz, dx, 1), device_id_type=MESH
            )
        )
        second[-1].start()

    relays = []

    def pass_on(*steps):
        for step in steps:
            arrived(sib, ss, rs, step).wait_recv()
            relays.append(relay(sib, ss, rs, step))
            relays[-1].start()

    for step in range(1, SIDE):
        arrived(gcv, sg, rg, step).wait_recv()
        relays.append(relay(gcv, sg, rg, step))
        relays[-1].start()

    for c in siblings:
        c.start()

    @pl.loop(2, 8)
    def _(leaf):
        near(leaf)

    def from_twin(buf, send, recv, step):
        at = 0 if step == 0 else SIDE - 1 + step
        source = lax.rem(twin[1] + NARROW - 2 * step, NARROW)
        return pltpu.make_async_remote_copy(
            buf.at[source], buf.at[source], send.at[at], recv.at[at], device_id=twin, device_id_type=MESH
        )

    for step in range(SIDE):
        from_twin(gcv, sg, rg, step).wait_recv()

    @pl.loop(0, NARROW)
    def _(j):
        rows = pl.ds(pl.multiple_of(j * RANK, RANK), RANK)
        gch[rows, :], gcl[rows, :] = split(gcv[j, :RANK, :])

    for i, (dz, dx) in enumerate(OFFSETS):
        source = far(dz, dx, -1)[0]
        pltpu.make_async_remote_copy(
            bbuf.at[source], bbuf.at[source], sb.at[i], rb_.at[i], device_id=far(dz, dx, 1), device_id_type=MESH
        ).wait_recv()

    picked = []
    for j in range(NARROW):
        tag = jnp.concatenate([gcv[j, RANK:, :]] * (SLICE // 8), axis=0)
        value = bbuf[0]
        for g in range(1, WIDE):
            value = jnp.where(tag == float(g), bbuf[g], value)
        picked.append(value)
    high, low = split(jnp.concatenate(picked, axis=1))
    both = dot(jnp.concatenate([high, low], axis=0), gch[...])
    part = both[:SLICE] + both[SLICE:] + dot(high, gcl[...])
    mine = pl.ds(pl.multiple_of(n * SLICE, SLICE), SLICE)
    cbuf[mine, :] = part
    third = []
    for d in range(1, NARROW):
        third.append(
            pltpu.make_async_remote_copy(
                cbuf.at[mine], cbuf.at[mine], sc.at[d - 1], rc.at[d - 1], device_id=mate(d), device_id_type=MESH
            )
        )
        third[-1].start()

    @pl.loop(0, REACH * PIECES)
    def _(i):
        for c in halo(i):
            c.wait_recv()

    for slot in (0, 1, REACH + LEAVES, REACH + LEAVES + 1):
        prepare(slot)

    @pl.loop(LEAVES - 2 * REACH, LEAVES)
    def _(i):
        near(i)

    pass_on(1, 2, 3)

    for step in range(SIDE):
        from_twin(sib, ss, rs, step).wait_recv()
    node = jnp.zeros((NVEC, RANK), F32)
    for j in range(2):
        node += dot3(split(sib[jnp.clip(fn[0, j], 0, NARROW - 1)]), split(ncv[j]))
    outv[...] = node

    for d in range(1, NARROW):
        source = pl.ds(pl.multiple_of(lax.rem(n + NARROW - d, NARROW) * SLICE, SLICE), SLICE)
        pltpu.make_async_remote_copy(
            cbuf.at[source], cbuf.at[source], sc.at[d - 1], rc.at[d - 1], device_id=mate(d), device_id_type=MESH
        ).wait_recv()
    node = outv[...] + dot3(split(cbuf[...]), split(ndv[...]), ((1,), (1,)))
    high, low = split(node.T)
    nt_out[0:RANK], nt_out[RANK : 2 * RANK], nt_out[2 * RANK :] = high, high, low

    for c in first + second + third + groups + siblings + relays:
        c.wait_send()

    @pl.loop(0, REACH * PIECES)
    def _(i):
        for c in halo(i):
            c.wait_send()


def finish(near, mm, nt, out, buf, sem):
    def done(leaf):
        return pltpu.make_async_copy(buf.at[leaf], out.at[leaf], sem.at[leaf])

    @pl.loop(0, LEAVES, unroll=12)
    def _(leaf):
        far = dot(mm[leaf], nt[: 2 * RANK]) + dot(mm[leaf, :, :RANK], nt[2 * RANK :])
        buf[leaf] = near[leaf] + far
        done(leaf).start()

    @pl.loop(0, LEAVES)
    def _(leaf):
        done(leaf).wait()


def shards(cot, rb, cb, lu, nu, nc, gc, nd, ld, nb, ni, fn, fg):
    hbm = pl.BlockSpec(memory_space=pltpu.HBM)
    vmem = pl.BlockSpec(memory_space=pltpu.VMEM)
    dma = pltpu.SemaphoreType.DMA
    shape = jax.ShapeDtypeStruct
    parts = pl.pallas_call(
        exchange,
        out_shape=[
            pltpu.VMEM((LEAVES, PTS, NVEC), F32),
            pltpu.VMEM((LEAVES, PTS, 2 * RANK), BF16),
            pltpu.VMEM((3 * RANK, NVEC), BF16),
        ],
        in_specs=[hbm] * 12 + [pl.BlockSpec(memory_space=pltpu.SMEM)],
        out_specs=[vmem] * 3,
        scratch_shapes=[
            pltpu.VMEM((LEAVES + 2 * REACH, PTS, NVEC), F32),
            pltpu.VMEM((LEAVES, PTS, RANK), F32),
            pltpu.VMEM((LEAVES, PTS, RANK), F32),
            pltpu.VMEM((LEAVES, RANK, RANK), F32),
            pltpu.VMEM((RANK, RANK), F32),
            pltpu.VMEM((2, RANK, RANK), F32),
            pltpu.VMEM((NARROW, RANK + 8, RANK), F32),
            pltpu.VMEM((RANK, RANK), F32),
            pltpu.VMEM((LEAVES, RANK, RANK), F32),
            pltpu.VMEM((LEAVES, NNEAR, PTS, PTS), F32),
            pltpu.VMEM((LEAVES + 2 * REACH, NVEC, PTS), BF16),
            pltpu.VMEM((LEAVES + 2 * REACH, NVEC, PTS), BF16),
            pltpu.VMEM((RANK, NVEC), F32),
            pltpu.VMEM((NVEC, RANK), F32),
            pltpu.VMEM((NARROW, NVEC, RANK), F32),
            pltpu.VMEM((NARROW - 1, SLICE, RANK), F32),
            pltpu.VMEM((WIDE, SLICE, RANK), F32),
            pltpu.VMEM((NVEC, RANK), F32),
            pltpu.VMEM((NVEC, RANK), F32),
            pltpu.VMEM((NARROW * RANK, RANK), BF16),
            pltpu.VMEM((NARROW * RANK, RANK), BF16),
            pltpu.SMEM((NNEAR, LEAVES), jnp.int32),
            pltpu.SMEM((1, 2), jnp.int32),
            dma((3, CHUNKS)),
            dma((4,)),
            dma((2,)),
            dma((LEAVES,)),
            dma((NARROW - 1,)),
            dma((NARROW - 1,)),
            dma((WIDE - 1,)),
            dma((WIDE - 1,)),
            dma((NARROW - 1,)),
            dma((NARROW - 1,)),
            dma((2 * SIDE - 1,)),
            dma((2 * SIDE - 1,)),
            dma((2 * SIDE - 1,)),
            dma((2 * SIDE - 1,)),
            dma((2, REACH * PIECES)),
            dma((2, REACH * PIECES)),
            dma((2,)),
        ],
        compiler_params=pltpu.CompilerParams(
            collective_id=0, has_side_effects=True, vmem_limit_bytes=48 * 2**20
        ),
    )(*[pltpu.with_memory_space_constraint(a, pltpu.HBM) for a in (cot, rb, cb, lu, nu, nc, gc, nd, ld, nb, ni.T, fn)], fg)
    return pl.pallas_call(
        finish,
        out_shape=shape((LEAVES, PTS, NVEC), F32),
        in_specs=[vmem] * 3,
        out_specs=hbm,
        scratch_shapes=[pltpu.VMEM((LEAVES, PTS, NVEC), F32), dma((LEAVES,))],
        compiler_params=pltpu.CompilerParams(vmem_limit_bytes=24 * 2**20),
    )(*parts)


def solution(mesh):
    leaf, both = P(("wide", "narrow"), None, None), P(("wide", "narrow"), None)
    wide4 = P(("wide", "narrow"), None, None, None)
    in_specs = (
        leaf, leaf, leaf, leaf, leaf, wide4, P("wide", "narrow", None, None), leaf, leaf, wide4,
        both, both, P("wide", "narrow"),
    )
    return jax.shard_map(shards, mesh=mesh, in_specs=in_specs, out_specs=leaf, check_vma=False)
```

```python
import functools

import jax
import jax.numpy as jnp
from jax import lax
from jax.experimental import pallas as pl
from jax.experimental.pallas import tpu as pltpu
from jax.sharding import PartitionSpec as P

MESH = pl.DeviceIdType.MESH
F32, BF16 = jnp.float32, jnp.bfloat16
LEAVES, PTS, RANK, NVEC = 12, 256, 128, 256
REACH, NNEAR = 2, 4
PIECES = 1
CHUNK = 6
CHUNKS = LEAVES // CHUNK
AHEAD = 3
PIECE = PTS // PIECES
WIDE, NARROW, SIDE = 16, 8, 4
SLICE = NVEC // NARROW
OFFSETS = [(dz, dx) for dz in (2, 1, 3, 0) for dx in (2, 1, 3, 0) if dz or dx]


def split(value):
    high = value.astype(BF16)
    return high, (value - high.astype(F32)).astype(BF16)


def dot(a, b, dims=((1,), (0,))):
    return lax.dot_general(a, b, (dims, ((), ())), preferred_element_type=F32)


def dot3(a, b, dims=((1,), (0,))):
    (ah, al), (bh, bl) = a, b
    return dot(ah, bh, dims) + (dot(al, bh, dims) + dot(ah, bl, dims))


def exchange(
    cot, rb, cb, lu, nu, nc, gc, nd, ld, nb, ni_hbm, fn_hbm, fg,
    near_out, mm_out, nt_out,
    cotv, rbv, cbv, luv, nuv, ncv, gcv, ndv, ldv, nbv,
    cth, ctl, up_sum, upv, sib, abuf, bbuf, cbuf, outv, gch, gcl, ni, fn,
    leaf_sem, small_sem, cb_sem, nb_sem,
    sa, ra, sb, rb_, sc, rc, ss, rs, sg, rg, sh, rh, int_sem,
):
    w, n = lax.axis_index("wide"), lax.axis_index("narrow")
    core = lax.rem(n, 2)

    def mate(d):
        return w, lax.rem(n + d, NARROW)

    def far(dz, dx, sign):
        z = lax.rem(w // SIDE + SIDE + sign * dz, SIDE)
        x = lax.rem(lax.rem(w, SIDE) + SIDE + sign * dx, SIDE)
        return z * SIDE + x, n

    rank = w * NARROW + n
    after, before = lax.rem(rank + 1, WIDE * NARROW), lax.rem(rank + WIDE * NARROW - 1, WIDE * NARROW)
    after, before = (after // NARROW, lax.rem(after, NARROW)), (before // NARROW, lax.rem(before, NARROW))

    barrier = pltpu.get_barrier_semaphore()
    for dz, dx in OFFSETS:
        pl.semaphore_signal(barrier, inc=1, device_id=far(dz, dx, 1), device_id_type=MESH)
    for d in range(1, NARROW):
        pl.semaphore_signal(barrier, inc=1, device_id=mate(d), device_id_type=MESH)
    for to in (after, before):
        pl.semaphore_signal(barrier, inc=1, device_id=to, device_id_type=MESH)

    def chunk_copies(chunk):
        at = pl.ds(chunk * CHUNK, CHUNK)
        return [
            pltpu.make_async_copy(rb.at[at], rbv.at[at], leaf_sem.at[0, chunk]),
            pltpu.make_async_copy(lu.at[at], luv.at[at], leaf_sem.at[1, chunk]),
            pltpu.make_async_copy(cot.at[at], cotv.at[pl.ds(REACH + chunk * CHUNK, CHUNK)], leaf_sem.at[2, chunk]),
        ]

    def near_copy(i):
        leaf = lax.rem(i + REACH, LEAVES)
        return pltpu.make_async_copy(nb.at[leaf], nbv.at[leaf], nb_sem.at[leaf])

    for chunk in range(2):
        for c in chunk_copies(chunk):
            c.start()

    smalls = [
        pltpu.make_async_copy(nu.at[0], nuv, small_sem.at[0]),
        pltpu.make_async_copy(gc.at[0, 0], gcv.at[n, pl.ds(0, RANK)], small_sem.at[1]),
        pltpu.make_async_copy(nc.at[0], ncv, small_sem.at[2]),
        pltpu.make_async_copy(nd.at[0], ndv, small_sem.at[3]),
    ]
    ints = [
        pltpu.make_async_copy(a, b, int_sem.at[i])
        for i, (a, b) in enumerate(((ni_hbm, ni), (fn_hbm, fn)))
    ]
    for c in smalls + ints:
        c.start()
    for c in ints:
        c.wait()

    gcv[n, RANK:, :] = jnp.full((8, RANK), fg[0, 0].astype(F32), F32)
    up_sum[...] = jnp.zeros_like(up_sum)

    def prepare(slot):
        cth[slot], ctl[slot] = split(cotv[slot].T)

    late = [pltpu.make_async_copy(cb, cbv, cb_sem.at[0]), pltpu.make_async_copy(ld, ldv, cb_sem.at[1])]

    @pl.loop(0, CHUNKS)
    def _(chunk):
        for c in chunk_copies(chunk):
            c.wait()

        @pl.when(chunk < CHUNKS - 2)
        def _():
            for c in chunk_copies(chunk + 2):
                c.start()

        @pl.when(chunk == CHUNKS - 2)
        def _():
            for i in range(AHEAD):
                near_copy(i).start()

        @pl.when(chunk == CHUNKS - 1)
        def _():
            for c in late:
                c.start()

        total = None
        for i in range(CHUNK):
            leaf = chunk * CHUNK + i
            lh, ll = split(luv[leaf].T)
            bh, bl = split(rbv[leaf])
            stacked = dot(jnp.concatenate([lh, ll], axis=0), bh, ((1,), (1,)))
            basis = stacked[:RANK] + stacked[RANK:] + dot(lh, bl, ((1,), (1,)))
            bh, bl = split(basis)
            ch, cl = split(cotv[REACH + leaf])
            stacked = dot(jnp.concatenate([bh, bl], axis=0), ch)
            term = stacked[:RANK] + stacked[RANK:] + dot(bh, cl)
            total = term if total is None else total + term
        up_sum[...] += total

    coeffs = up_sum[...].T
    sib[n] = coeffs
    for c in smalls:
        c.wait()
    upv[...] = dot3(split(coeffs), split(nuv[...]))

    pl.semaphore_wait(barrier, len(OFFSETS) + NARROW + 1)

    first = []
    for d in range(1, NARROW):
        to = mate(d)
        first.append(
            pltpu.make_async_remote_copy(
                upv.at[pl.ds(pl.multiple_of(to[1] * SLICE, SLICE), SLICE)], abuf.at[d - 1],
                sa.at[d - 1], ra.at[d - 1], device_id=to, device_id_type=MESH,
            )
        )
        first[-1].start()

    twin = (w, n + 1 - 2 * core)

    def spread(buf, send, recv):
        out = []
        for step in range(SIDE):
            to = twin if step == 0 else mate(2 * step)
            out.append(
                pltpu.make_async_remote_copy(
                    buf.at[n], buf.at[n], send.at[step], recv.at[step], device_id=to, device_id_type=MESH
                )
            )
        return out

    def arrived(buf, send, recv, step):
        source = lax.rem(n + NARROW - 2 * step, NARROW)
        return pltpu.make_async_remote_copy(
            buf.at[source], buf.at[source], send.at[step], recv.at[step], device_id=twin, device_id_type=MESH
        )

    def relay(buf, send, recv, step):
        source = lax.rem(n + NARROW - 2 * step, NARROW)
        return pltpu.make_async_remote_copy(
            buf.at[source], buf.at[source], send.at[SIDE - 1 + step], recv.at[SIDE - 1 + step],
            device_id=twin, device_id_type=MESH,
        )

    groups = spread(gcv, sg, rg)
    siblings = spread(sib, ss, rs)

    def halo(i):
        leaf, rows = i // PIECES, pl.ds(pl.multiple_of(lax.rem(i, PIECES) * PIECE, PIECE), PIECE)
        return [
            pltpu.make_async_remote_copy(
                cot.at[LEAVES - REACH + leaf, rows], cotv.at[leaf, rows],
                sh.at[0, i], rh.at[0, i], device_id=after, device_id_type=MESH,
            ),
            pltpu.make_async_remote_copy(
                cot.at[leaf, rows], cotv.at[REACH + LEAVES + leaf, rows],
                sh.at[1, i], rh.at[1, i], device_id=before, device_id_type=MESH,
            ),
        ]

    def send_halo(low, high):
        @pl.loop(low, high)
        def _(i):
            for c in halo(i):
                c.start()

    def merge_down():
        for c in late:
            c.wait()

        @pl.loop(0, LEAVES, unroll=2)
        def _(leaf):
            wh, wl = split(ldv[leaf])
            row = jnp.concatenate([wh, wl], axis=1)
            both = dot(jnp.concatenate(split(cbv[leaf]), axis=1), jnp.concatenate([row, row], axis=0))
            mm_out[leaf] = jnp.concatenate(split(both[:, :RANK] + both[:, RANK:]), axis=1)

    send_halo(0, 2)

    for c in groups:
        c.start()

    @pl.loop(0, LEAVES, unroll=2)
    def _(leaf):
        prepare(REACH + leaf)

    first_leaf = rank * LEAVES - REACH

    def near(i):
        leaf = lax.rem(i + REACH, LEAVES)
        near_copy(i).wait()

        @pl.when(i + AHEAD < LEAVES)
        def _():
            near_copy(i + AHEAD).start()

        total = None
        for j in range(NNEAR):
            source = jnp.clip(ni[j, leaf] - first_leaf, 0, LEAVES + 2 * REACH - 1)
            term = dot3((cth[source], ctl[source]), split(nbv[leaf, j]))
            total = term if total is None else total + term
        near_out[leaf] = total.T

    @pl.loop(0, 2)
    def _(leaf):
        near(leaf)

    merge_down()

    own = upv[pl.ds(pl.multiple_of(n * SLICE, SLICE), SLICE), :]
    for d, c in enumerate(first):
        c.wait_recv()
        own += abuf[d]
    bbuf[w] = own
    second = []
    for i, (dz, dx) in enumerate(OFFSETS):
        second.append(
            pltpu.make_async_remote_copy(
                bbuf.at[w], bbuf.at[w], sb.at[i], rb_.at[i], device_id=far(dz, dx, 1), device_id_type=MESH
            )
        )
        second[-1].start()

    relays = []

    def pass_on(*steps):
        for step in steps:
            arrived(sib, ss, rs, step).wait_recv()
            relays.append(relay(sib, ss, rs, step))
            relays[-1].start()

    for step in range(1, SIDE):
        arrived(gcv, sg, rg, step).wait_recv()
        relays.append(relay(gcv, sg, rg, step))
        relays[-1].start()

    for c in siblings:
        c.start()

    @pl.loop(2, 8)
    def _(leaf):
        near(leaf)

    def from_twin(buf, send, recv, step):
        at = 0 if step == 0 else SIDE - 1 + step
        source = lax.rem(twin[1] + NARROW - 2 * step, NARROW)
        return pltpu.make_async_remote_copy(
            buf.at[source], buf.at[source], send.at[at], recv.at[at], device_id=twin, device_id_type=MESH
        )

    for step in range(SIDE):
        from_twin(gcv, sg, rg, step).wait_recv()

    @pl.loop(0, NARROW)
    def _(j):
        rows = pl.ds(pl.multiple_of(j * RANK, RANK), RANK)
        gch[rows, :], gcl[rows, :] = split(gcv[j, :RANK, :])

    for i, (dz, dx) in enumerate(OFFSETS):
        source = far(dz, dx, -1)[0]
        pltpu.make_async_remote_copy(
            bbuf.at[source], bbuf.at[source], sb.at[i], rb_.at[i], device_id=far(dz, dx, 1), device_id_type=MESH
        ).wait_recv()

    picked = []
    for j in range(NARROW):
        tag = jnp.concatenate([gcv[j, RANK:, :]] * (SLICE // 8), axis=0)
        value = bbuf[0]
        for g in range(1, WIDE):
            value = jnp.where(tag == float(g), bbuf[g], value)
        picked.append(value)
    high, low = split(jnp.concatenate(picked, axis=1))
    both = dot(jnp.concatenate([high, low], axis=0), gch[...])
    part = both[:SLICE] + both[SLICE:] + dot(high, gcl[...])
    mine = pl.ds(pl.multiple_of(n * SLICE, SLICE), SLICE)
    cbuf[mine, :] = part
    third = []
    for d in range(1, NARROW):
        third.append(
            pltpu.make_async_remote_copy(
                cbuf.at[mine], cbuf.at[mine], sc.at[d - 1], rc.at[d - 1], device_id=mate(d), device_id_type=MESH
            )
        )
        third[-1].start()

    @pl.loop(0, REACH * PIECES)
    def _(i):
        for c in halo(i):
            c.wait_recv()

    for slot in (0, 1, REACH + LEAVES, REACH + LEAVES + 1):
        prepare(slot)

    @pl.loop(LEAVES - 2 * REACH, LEAVES)
    def _(i):
        near(i)

    pass_on(1, 2, 3)

    for step in range(SIDE):
        from_twin(sib, ss, rs, step).wait_recv()
    node = jnp.zeros((NVEC, RANK), F32)
    for j in range(2):
        node += dot3(split(sib[jnp.clip(fn[0, j], 0, NARROW - 1)]), split(ncv[j]))
    outv[...] = node

    down = split(ndv[...])
    for d in range(1, NARROW):
        source = pl.ds(pl.multiple_of(lax.rem(n + NARROW - d, NARROW) * SLICE, SLICE), SLICE)
        pltpu.make_async_remote_copy(
            cbuf.at[source], cbuf.at[source], sc.at[d - 1], rc.at[d - 1], device_id=mate(d), device_id_type=MESH
        ).wait_recv()
    node = outv[...] + dot3(split(cbuf[...]), down, ((1,), (1,)))
    high, low = split(node.T)
    nt_out[0:RANK], nt_out[RANK : 2 * RANK], nt_out[2 * RANK :] = high, high, low

    for c in first + second + third + groups + siblings + relays:
        c.wait_send()

    @pl.loop(0, REACH * PIECES)
    def _(i):
        for c in halo(i):
            c.wait_send()


def finish(near, mm, nt, out, buf, sem):
    def done(leaf):
        return pltpu.make_async_copy(buf.at[leaf], out.at[leaf], sem.at[leaf])

    @pl.loop(0, LEAVES, unroll=12)
    def _(leaf):
        far = dot(mm[leaf], nt[: 2 * RANK]) + dot(mm[leaf, :, :RANK], nt[2 * RANK :])
        buf[leaf] = near[leaf] + far
        done(leaf).start()

    @pl.loop(0, LEAVES)
    def _(leaf):
        done(leaf).wait()


def shards(cot, rb, cb, lu, nu, nc, gc, nd, ld, nb, ni, fn, fg):
    hbm = pl.BlockSpec(memory_space=pltpu.HBM)
    vmem = pl.BlockSpec(memory_space=pltpu.VMEM)
    dma = pltpu.SemaphoreType.DMA
    shape = jax.ShapeDtypeStruct
    parts = pl.pallas_call(
        exchange,
        out_shape=[
            pltpu.VMEM((LEAVES, PTS, NVEC), F32),
            pltpu.VMEM((LEAVES, PTS, 2 * RANK), BF16),
            pltpu.VMEM((3 * RANK, NVEC), BF16),
        ],
        in_specs=[hbm] * 12 + [pl.BlockSpec(memory_space=pltpu.SMEM)],
        out_specs=[vmem] * 3,
        scratch_shapes=[
            pltpu.VMEM((LEAVES + 2 * REACH, PTS, NVEC), F32),
            pltpu.VMEM((LEAVES, PTS, RANK), F32),
            pltpu.VMEM((LEAVES, PTS, RANK), F32),
            pltpu.VMEM((LEAVES, RANK, RANK), F32),
            pltpu.VMEM((RANK, RANK), F32),
            pltpu.VMEM((2, RANK, RANK), F32),
            pltpu.VMEM((NARROW, RANK + 8, RANK), F32),
            pltpu.VMEM((RANK, RANK), F32),
            pltpu.VMEM((LEAVES, RANK, RANK), F32),
            pltpu.VMEM((LEAVES, NNEAR, PTS, PTS), F32),
            pltpu.VMEM((LEAVES + 2 * REACH, NVEC, PTS), BF16),
            pltpu.VMEM((LEAVES + 2 * REACH, NVEC, PTS), BF16),
            pltpu.VMEM((RANK, NVEC), F32),
            pltpu.VMEM((NVEC, RANK), F32),
            pltpu.VMEM((NARROW, NVEC, RANK), F32),
            pltpu.VMEM((NARROW - 1, SLICE, RANK), F32),
            pltpu.VMEM((WIDE, SLICE, RANK), F32),
            pltpu.VMEM((NVEC, RANK), F32),
            pltpu.VMEM((NVEC, RANK), F32),
            pltpu.VMEM((NARROW * RANK, RANK), BF16),
            pltpu.VMEM((NARROW * RANK, RANK), BF16),
            pltpu.SMEM((NNEAR, LEAVES), jnp.int32),
            pltpu.SMEM((1, 2), jnp.int32),
            dma((3, CHUNKS)),
            dma((4,)),
            dma((2,)),
            dma((LEAVES,)),
            dma((NARROW - 1,)),
            dma((NARROW - 1,)),
            dma((WIDE - 1,)),
            dma((WIDE - 1,)),
            dma((NARROW - 1,)),
            dma((NARROW - 1,)),
            dma((2 * SIDE - 1,)),
            dma((2 * SIDE - 1,)),
            dma((2 * SIDE - 1,)),
            dma((2 * SIDE - 1,)),
            dma((2, REACH * PIECES)),
            dma((2, REACH * PIECES)),
            dma((2,)),
        ],
        compiler_params=pltpu.CompilerParams(
            collective_id=0, has_side_effects=True, vmem_limit_bytes=48 * 2**20
        ),
    )(*[pltpu.with_memory_space_constraint(a, pltpu.HBM) for a in (cot, rb, cb, lu, nu, nc, gc, nd, ld, nb, ni.T, fn)], fg)
    return pl.pallas_call(
        finish,
        out_shape=shape((LEAVES, PTS, NVEC), F32),
        in_specs=[vmem] * 3,
        out_specs=hbm,
        scratch_shapes=[pltpu.VMEM((LEAVES, PTS, NVEC), F32), dma((LEAVES,))],
        compiler_params=pltpu.CompilerParams(vmem_limit_bytes=24 * 2**20),
    )(*parts)


def solution(mesh):
    leaf, both = P(("wide", "narrow"), None, None), P(("wide", "narrow"), None)
    wide4 = P(("wide", "narrow"), None, None, None)
    in_specs = (
        leaf, leaf, leaf, leaf, leaf, wide4, P("wide", "narrow", None, None), leaf, leaf, wide4,
        both, both, P("wide", "narrow"),
    )
    return jax.shard_map(shards, mesh=mesh, in_specs=in_specs, out_specs=leaf, check_vma=False)
```
